32 devices in a mesh: gx: 4 (over y, core), gy: 8 (over z, x).
Axes of the slice: x: 2, y: 2, z: 4, core: 2. Of those that a mesh axis runs over, the one named last changes fastest.
Arguments:
- slope_depth: float32 [1024, 4096], P('gx', 'gy'), may hold values from 0.2 to 2
- slope_momentum: float32 [2, 1024, 4096], P(None, 'gx', 'gy'), may hold values from -1.2 to 1.2
- bed_slope: float32 [2, 1024, 4096], P(None, 'gx', 'gy'), may hold values from -3 to 3
- friction: float32 [1024, 4096], P('gx', 'gy'), may hold values from 0.2 to 2
- slope_active: int32 [1024, 4096], P('gx', 'gy'), may hold values 0 or 1
- owners: int32 [4, 8, 256, 1], P('gx', 'gy'), may hold values from 0 to 31; in each aligned block of 256 rows (0 to 255, 256 to 511, ..., all dimensions but the last counted through in order) at most 16 rows name the same one
- offsets: int32 [4, 8, 256], P('gx', 'gy'), may hold values from 0 to 511
- lake_height: float32 [2048, 4096], P('gx', 'gy'), may hold values from -6 to 6
- lake_momentum: float32 [2, 2048, 4096], P(None, 'gx', 'gy'), may hold values from -16 to 16
- lake_diagonal: float32 [2048, 4096], P('gx', 'gy'), may hold values from 0.2 to 2
Outputs:
- slope_fields: float32 [3, 1024, 4096], P(None, 'gx', 'gy')
- new_height: float32 [2048, 4096], P('gx', 'gy')
- new_momentum: float32 [2, 2048, 4096], P(None, 'gx', 'gy')
The draws below stay inside these ranges and needn't reach their ends.
Inputs may be any that keep to these rules, and one draw needn't show every extreme that they name: `owners`: among the 256 rows of one device, no owner is named by more than 16 rows, a bound that some block reaches.
All inputs are finite; a program needn't handle non-finite values. No bound on the sum of `slope_active` on one device may be relied on, other than what follows from the above.
Results may differ from the reference program's by a relative error of at most 0.0001.
Values sent between devices are 32-bit elements; how exact they have to be, the bound alone decides.
A program may use at most 128 MiB of HBM per device.

```python
import math
import jax
import jax.numpy as jnp
import numpy as np

CX = 256
CY = 512
LX = 512
SECTIONS = 2
ITERS = 3
CAP = 16
SLOPE_ROWS = 1024
LAKE_ROWS = 2048
GRID_COLS = 4096
N_GX = 4
N_GY = 8
DEVICES = 32


def draw_lake_momentum(key, part):
    first_key = jax.random.fold_in(key, 0)
    row_frac = jnp.arange(LAKE_ROWS, dtype=jnp.float32) / LAKE_ROWS
    row_scale = 0.6 + 0.6 * row_frac
    normal_part = jnp.clip(jax.random.normal(first_key, (2, LAKE_ROWS, GRID_COLS), jnp.float32), -4.0, 4.0)
    return normal_part * row_scale[None, :, None]


def set_ends(result, key, smallest, top_value):
    dims = result.shape
    place = [jax.random.randint(jax.random.fold_in(key, axis), (), 0, dims[axis]) for axis in range(len(dims))]
    result = result.at[tuple(place)].set(smallest)
    longest = dims.index(max(dims))
    place[longest] = (place[longest] + 1) % dims[longest]
    return result.at[tuple(place)].set(top_value)


def shard_levels(key, shape, shards, low, high):
    loudness, own = 1.0, jax.random.fold_in(key, 6)
    for dim, parts in shards:
        heights = jnp.exp(jax.random.uniform(jax.random.fold_in(own, dim), (parts,), jnp.float32, low / len(shards), high / len(shards)))
        loudness = loudness * jnp.repeat(heights, shape[dim] // parts).reshape([-1 if axis == dim else 1 for axis in range(len(shape))])
    return loudness


def shared_out(own_key, own, number, rows, amount, top, most, lean):
    ranking = jax.random.permutation(own_key, amount)
    heavy_load, ordinary = portions_of(amount, rows * top, most, lean, True), portions_of(amount, rows * top, most, lean, False)
    places = jnp.arange(amount)

    def named(lengths, rotation):
        used = int((lengths > 0).sum())
        fixed = max(1, used // 4)
        shifted = fixed + (places - fixed + rotation * (used - fixed)) % max(1, amount - fixed)
        return jnp.zeros((amount,), jnp.int32).at[ranking[jnp.where(places < fixed, places, shifted)]].set(jnp.asarray(lengths, jnp.int32))

    lengths = jnp.where(number % 4 == 0, named(heavy_load, number // 4), named(ordinary, number - number // 4 - 1))
    mixed = jax.random.permutation(jax.random.fold_in(own, 3), amount)
    donor, taker = mixed[0:amount // 2 * 2:2], mixed[1:amount // 2 * 2:2]
    margin = jnp.minimum(lengths[donor] - 1, most - lengths[taker]) // 2
    margin = jnp.where((donor == ranking[0]) | (taker == ranking[0]) | (lengths[taker] == 0), 0, jnp.maximum(margin, 0))
    shifted = jax.random.randint(jax.random.fold_in(own, 4), (amount // 2,), 0, 1 << 20) % (margin + 1)
    lengths = lengths.at[donor].add(-shifted).at[taker].add(shifted)
    members = jnp.searchsorted(jnp.cumsum(lengths), jnp.arange(rows * top), side="right").astype(jnp.int32)
    listing = members.reshape(top, rows).T
    listing = listing[jax.random.permutation(jax.random.fold_in(own, 1), rows)]
    rotation = jax.random.randint(jax.random.fold_in(own, 2), (rows, 1), 0, top)
    return jnp.take_along_axis(listing, (jnp.arange(top)[None, :] + rotation) % top, axis=1)


def portions_of(count, total, bound, slope, full):
    portions = [(1 << 20) // math.isqrt(grade ** slope) + 1 for grade in range(1, count + 1)]
    largest = bound if full else min(bound, max(-(-total // count), total * portions[0] // sum(portions)))
    least = 1 if total - largest >= count - 1 else 0
    given, rest = [largest] + [least] * (count - 1), total - largest - least * (count - 1)
    while rest > 0:
        free = [i for i in range(1, count) if given[i] < largest] or [i for i in range(1, count) if given[i] < bound]
        pool, remaining = sum([portions[i] for i in free]), rest
        for i in free:
            more = min(bound - given[i], max(1, remaining * portions[i] // pool), rest)
            given[i] = given[i] + more
            rest = rest - more
    return np.array(given)


def gaussian(rng, extent, scale, bound, pieces=(), held_as=jnp.bfloat16):
    entries = jax.random.normal(rng, extent, jnp.float32) * scale
    if len(pieces) > 0:
        entries = shard_levels(rng, extent, pieces, -0.22, 0.18) * entries
    return jnp.clip(entries, min=-bound, max=bound).astype(held_as)


def setup_inputs(seed: int = 0) -> dict:
    arg_keys = jax.random.split(jax.random.key(seed), 11)
    slope_depth = jnp.clip(jnp.exp(math.log(2.0) - 2.3025851 * jax.random.uniform(arg_keys[0], (SLOPE_ROWS, GRID_COLS), jnp.float32) ** shard_levels(arg_keys[0], (SLOPE_ROWS, GRID_COLS), ((0, 4), (1, 8)), -0.2, 0.2)), 0.2, 2.0)
    slope_momentum = gaussian(arg_keys[1], (2, SLOPE_ROWS, GRID_COLS), 0.3, 1.2, ((1, 4), (2, 8)), jnp.float32)
    bed_slope = gaussian(arg_keys[2], (2, SLOPE_ROWS, GRID_COLS), 0.5, 3.0, ((1, 4), (2, 8)), jnp.float32)
    friction = jnp.clip(jnp.exp(math.log(2.0) - 2.3025851 * jax.random.uniform(arg_keys[3], (SLOPE_ROWS, GRID_COLS), jnp.float32) ** shard_levels(arg_keys[3], (SLOPE_ROWS, GRID_COLS), ((0, 4), (1, 8)), -0.2, 0.2)), 0.2, 2.0)
    slope_active = set_ends((jax.random.randint(arg_keys[4], (SLOPE_ROWS, GRID_COLS), 0, 4) < 3).astype(jnp.int32), jax.random.fold_in(arg_keys[4], 1), 0, 1)
    owners_keys = jax.random.split(jax.random.fold_in(arg_keys[5], 1), N_GX * N_GY * CX // CX)
    owners_turns = jax.random.permutation(jax.random.fold_in(arg_keys[5], 3), N_GX * N_GY * CX // CX)
    owners = jax.vmap(lambda own, number: shared_out(jax.random.fold_in(arg_keys[5], 2), own, number, CX, DEVICES, 1, CAP, 2))(owners_keys, owners_turns).reshape((N_GX, N_GY, CX, 1))
    offsets = set_ends(jax.random.randint(arg_keys[6], (N_GX, N_GY, CX), 0, LX), jax.random.fold_in(arg_keys[6], 1), 0, LX - 1).astype(jnp.int32)
    lake_height = gaussian(arg_keys[7], (LAKE_ROWS, GRID_COLS), 1.0, 6.0, ((0, 4), (1, 8)), jnp.float32)
    lake_momentum = draw_lake_momentum(jax.random.fold_in(arg_keys[10], 71), 0)
    lake_diagonal = jnp.clip(0.2 + 1.8 * jax.random.uniform(arg_keys[9], (LAKE_ROWS, GRID_COLS), jnp.float32) ** shard_levels(arg_keys[9], (LAKE_ROWS, GRID_COLS), ((0, 4), (1, 8)), -0.2, 0.2), 0.2, 2.0)
    return {"slope_depth": slope_depth, "slope_momentum": slope_momentum, "bed_slope": bed_slope, "friction": friction, "slope_active": slope_active, "owners": owners, "offsets": offsets, "lake_height": lake_height, "lake_momentum": lake_momentum, "lake_diagonal": lake_diagonal}


courant = 0.15
depth_floor = 0.25
dispersion = 0.5


def advance(fields, padded, bed_slope, friction, active):
    height = padded[0]
    floored = jnp.maximum(height, depth_floor)
    along_speed = padded[1] / floored
    across_speed = padded[2] / floored
    pressure = 0.5 * height * height
    flux_along = jnp.stack([padded[1], padded[1] * along_speed + pressure, padded[2] * along_speed])
    flux_across = jnp.stack([padded[2], padded[1] * across_speed, padded[2] * across_speed + pressure])
    average = 0.25 * (padded[:, 2:, 1:-1] + padded[:, :-2, 1:-1] + padded[:, 1:-1, 2:] + padded[:, 1:-1, :-2])
    update = average - 0.5 * courant * (flux_along[:, 2:, 1:-1] - flux_along[:, :-2, 1:-1])
    update = update - 0.5 * courant * (flux_across[:, 1:-1, 2:] - flux_across[:, 1:-1, :-2])
    forcing = jnp.stack([jnp.zeros_like(fields[0]), fields[0] * bed_slope[0] - friction * fields[1], fields[0] * bed_slope[1] - friction * fields[2]])
    return (update + courant * forcing) * active[None]


def operate(vectors, lake_diagonal):
    padded = jnp.pad(vectors, ((0, 0), (1, 1), (1, 1)))
    beside = padded[:, 2:, 1:-1] + padded[:, :-2, 1:-1] + padded[:, 1:-1, 2:] + padded[:, 1:-1, :-2]
    return (1.0 + 4.0 * dispersion + lake_diagonal)[None] * vectors - dispersion * beside


def reference(slope_depth, slope_momentum, bed_slope, friction, slope_active, owners, offsets, lake_height, lake_momentum, lake_diagonal):
    active = slope_active.astype(jnp.float32)
    fields = jnp.concatenate([slope_depth[None], slope_momentum], axis=0)
    for section_index in range(SECTIONS):
        padded = jnp.pad(fields, ((0, 0), (1, 1), (1, 1)))
        fields = advance(fields, padded, bed_slope, friction, active)
    blocks = fields.reshape(3, N_GX, CX, N_GY, CY).transpose(1, 3, 2, 0, 4).reshape(N_GX * N_GY * CX, 3, CY)
    owner_flat = owners.reshape(-1).astype(jnp.int32)
    offset_flat = offsets.reshape(-1).astype(jnp.int32)
    target = ((owner_flat // N_GY) * LX + offset_flat) * N_GY + owner_flat % N_GY
    inflow = jax.ops.segment_sum(blocks, target, num_segments=LAKE_ROWS * N_GY)
    inflow = inflow.reshape(LAKE_ROWS, N_GY, 3, CY).transpose(2, 0, 1, 3).reshape(3, LAKE_ROWS, GRID_COLS)
    new_height = lake_height + inflow[0]
    right_side = lake_momentum + inflow[1:]
    solution = jnp.zeros_like(right_side)
    residual = right_side
    direction = right_side
    norm_now = jnp.sum(residual * residual, axis=(1, 2))
    for iteration in range(ITERS):
        applied = operate(direction, lake_diagonal)
        step_length = norm_now / jnp.sum(direction * applied, axis=(1, 2))
        solution = solution + step_length[:, None, None] * direction
        residual = residual - step_length[:, None, None] * applied
        norm_next = jnp.sum(residual * residual, axis=(1, 2))
        direction = residual + (norm_next / norm_now)[:, None, None] * direction
        norm_now = norm_next
    return fields, new_height, solution
```

```python
import functools

import jax
import jax.numpy as jnp
from jax import lax
from jax.experimental import pallas as pl
from jax.experimental.pallas import tpu as pltpu
from jax.sharding import PartitionSpec as P

SECTIONS = 2
courant = 0.15
depth_floor = 0.25
dispersion = 0.5
SHIFT = 4.1
PAD = 8
MESH = pl.DeviceIdType.MESH


def along_terms(h, m, n, sign):
    inv = 1.0 / jnp.maximum(h, depth_floor)
    u = m * inv
    k = sign * 0.5 * courant
    return (0.25 * h + k * m, 0.25 * m + k * (m * u + 0.5 * h * h), 0.25 * n + k * (n * u))


def across_terms(h, m, n, sign):
    inv = 1.0 / jnp.maximum(h, depth_floor)
    v = n * inv
    k = sign * 0.5 * courant
    return (0.25 * h + k * n, 0.25 * m + k * (m * v), 0.25 * n + k * (n * v + 0.5 * h * h))


def split3(x):
    hi = x.astype(jnp.bfloat16)
    rest = x - hi.astype(jnp.float32)
    mid = rest.astype(jnp.bfloat16)
    low = (rest - mid.astype(jnp.float32)).astype(jnp.bfloat16)
    return hi, mid, low


def column(x, lane):
    return jnp.transpose(x)[lane : lane + 1, :]


def as_column(row):
    return jnp.transpose(jnp.broadcast_to(row, (128, row.shape[1])))


def kernel(
    n0,
    n1,
    cap,
    depth_ref,
    mom_ref,
    bed_ref,
    fric_ref,
    act_ref,
    own_row_ref,
    own_col_ref,
    off_ref,
    lh_hbm,
    lm_hbm,
    ld_hbm,
    slope_out,
    height_out,
    lake_out,
    fields,
    parts,
    send,
    recv,
    tag_send,
    tag_recv,
    hot,
    rparts,
    vec,
    lh,
    ld,
    srow_s,
    srow_r,
    scol_s,
    scol_r,
    lrow_s,
    lrow_r,
    lcol_s,
    lcol_r,
    sum_s,
    sum_r,
    tag_ss,
    tag_rs,
    blk_ss,
    blk_rs,
    sl_ss,
    sl_rs,
    lk_ss,
    lk_rs,
    sum_ss,
    sum_rs,
    loc,
):
    n = n0 * n1
    gx = lax.axis_index("gx")
    gy = lax.axis_index("gy")
    me = gx * n1 + gy
    rows, cols = depth_ref.shape
    lrows = lh.shape[0]
    slots = n * cap
    f32 = jnp.float32

    def peer(k):
        return lax.rem(me + k, n)

    def coords(t):
        return (lax.div(t, n1), lax.rem(t, n1))

    load_m = [
        pltpu.make_async_copy(lm_hbm.at[c], vec.at[0, c, pl.ds(PAD, lrows), :], loc.at[c])
        for c in range(2)
    ]
    load_h = pltpu.make_async_copy(lh_hbm, lh, loc.at[2])
    load_d = pltpu.make_async_copy(ld_hbm, ld, loc.at[3])
    for c in load_m + [load_h, load_d]:
        c.start()

    barrier = pltpu.get_barrier_semaphore()

    def greet(k, carry):
        pl.semaphore_signal(barrier, inc=1, device_id=coords(peer(k)), device_id_type=MESH)
        return carry

    lax.fori_loop(1, n, greet, 0)

    own_row = own_row_ref[...]
    before = lax.broadcasted_iota(jnp.int32, (rows, rows), 0) < lax.broadcasted_iota(
        jnp.int32, (rows, rows), 1
    )
    rank = jnp.sum(
        jnp.where((own_col_ref[...] == own_row) & before, 1.0, 0.0), axis=0, keepdims=True
    )
    slot = own_row * cap + rank.astype(jnp.int32)
    off = (off_ref[...] + 1).astype(f32)
    SC = 128

    def chosen(j):
        return (lax.broadcasted_iota(jnp.int32, (SC, rows), 0) + j * SC) == slot

    def tags(j, carry):
        col = jnp.sum(jnp.where(chosen(j), off, 0.0), axis=1, keepdims=True)
        tag_send[pl.ds(pl.multiple_of(j * SC, SC), SC), :] = jnp.broadcast_to(col, (SC, 128))
        return carry

    lax.fori_loop(0, slots // SC, tags, 0)

    for c in range(3):
        for e in range(SECTIONS):
            fields[e, c, 0:PAD, :] = jnp.zeros((PAD, cols), f32)
            fields[e, c, PAD + rows : PAD + rows + PAD, :] = jnp.zeros((PAD, cols), f32)
    for c in range(2):
        for e in range(3):
            vec[e, c, 0:PAD, :] = jnp.zeros((PAD, cols), f32)
            vec[e, c, PAD + lrows : PAD + lrows + PAD, :] = jnp.zeros((PAD, cols), f32)
    fields[0, 0, PAD : PAD + rows, :] = depth_ref[...]
    fields[0, 1, PAD : PAD + rows, :] = mom_ref[0]
    fields[0, 2, PAD : PAD + rows, :] = mom_ref[1]

    pl.semaphore_wait(barrier, n - 1)

    def at(t):
        return pl.ds(pl.multiple_of(t * cap, cap), cap)

    def tag_copy(t, s):
        return pltpu.make_async_remote_copy(
            src_ref=tag_send.at[at(t), :],
            dst_ref=tag_recv.at[at(s), :],
            send_sem=tag_ss.at[t],
            recv_sem=tag_rs.at[s],
            device_id=coords(t),
            device_id_type=MESH,
        )

    def blk_copy(t, s):
        return pltpu.make_async_remote_copy(
            src_ref=send.at[at(t), :],
            dst_ref=recv.at[at(s), :],
            send_sem=blk_ss.at[t],
            recv_sem=blk_rs.at[s],
            device_id=coords(t),
            device_id_type=MESH,
        )

    neighbours = (
        (lax.rem(gx + 1, n0), gy),
        (lax.rem(gx + n0 - 1, n0), gy),
        (gx, lax.rem(gy + 1, n1)),
        (gx, lax.rem(gy + n1 - 1, n1)),
    )
    there = (gx > 0, gx < n0 - 1, gy > 0, gy < n1 - 1)

    def halo_copies(e, row_s, row_r, col_s, col_r, ss, rs):
        out = []
        for d in range(4):
            s, r = (row_s, row_r) if d < 2 else (col_s, col_r)
            out.append(
                pltpu.make_async_remote_copy(
                    src_ref=s.at[e, d % 2],
                    dst_ref=r.at[e, d % 2],
                    send_sem=ss.at[e, d],
                    recv_sem=rs.at[e, d],
                    device_id=neighbours[d],
                    device_id_type=MESH,
                )
            )
        return out

    pending = []
    RB = 64
    lane = lax.broadcasted_iota(jnp.int32, (RB, cols), 1)
    first_lane = lane == 0
    last_lane = lane == cols - 1

    def from_left(x):
        return jnp.where(first_lane, 0.0, pltpu.roll(x, 1, 1))

    def from_right(x):
        return jnp.where(last_lane, 0.0, pltpu.roll(x, cols - 1, 1))

    for e in range(SECTIONS):
        lo = [fields[e, c, PAD : PAD + 8, :] for c in range(3)]
        hi = [fields[e, c, PAD + rows - 8 : PAD + rows, :] for c in range(3)]
        for c, x in enumerate(along_terms(*hi, 1.0)):
            srow_s[e, 0, c : c + 1, :] = x[7:8, :]
        for c, x in enumerate(along_terms(*lo, -1.0)):
            srow_s[e, 1, c : c + 1, :] = x[0:1, :]
        right = [fields[e, c, PAD : PAD + rows, cols - 128 : cols] for c in range(3)]
        for c, x in enumerate(across_terms(*right, 1.0)):
            scol_s[e, 0, c : c + 1, :] = column(x, 127)
        left = [fields[e, c, PAD : PAD + rows, 0:128] for c in range(3)]
        for c, x in enumerate(across_terms(*left, -1.0)):
            scol_s[e, 1, c : c + 1, :] = column(x, 0)
        copies = halo_copies(e, srow_s, srow_r, scol_s, scol_r, sl_ss, sl_rs)
        for c in copies:
            c.start()
        pending += copies
        if e == 0:

            def send_tags(k, carry):
                tag_copy(peer(k), me).start()
                return carry

            lax.fori_loop(1, n, send_tags, 0)

        def section(i, carry):
            base = pl.multiple_of(i * RB, RB)
            x = [fields[e, c, pl.ds(base, RB + 2 * PAD), :] for c in range(3)]
            mid = [v[PAD : PAD + RB, :] for v in x]
            below = along_terms(*[v[PAD - 1 : PAD - 1 + RB, :] for v in x], 1.0)
            above = along_terms(*[v[PAD + 1 : PAD + 1 + RB, :] for v in x], -1.0)
            left = across_terms(*mid, 1.0)
            right = across_terms(*mid, -1.0)
            here = pl.ds(base, RB)
            active = act_ref[here, :].astype(f32)
            fric = fric_ref[here, :]
            for c in range(3):
                total = below[c] + above[c] + from_left(left[c]) + from_right(right[c])
                if c > 0:
                    total = total + courant * (mid[0] * bed_ref[c - 1, here, :] - fric * mid[c])
                fields[e + 1, c, pl.ds(pl.multiple_of(base + PAD, PAD), RB), :] = total * active
            return carry

        lax.fori_loop(0, rows // RB, section, 0)
        for c in copies:
            c.wait_recv()
        sub = lax.broadcasted_iota(jnp.int32, (8, cols), 0)
        tile_lane = lax.broadcasted_iota(jnp.int32, (rows, 128), 1)
        for d, (r0, at_row) in enumerate(((0, 0), (rows - 8, 7))):
            act = act_ref[r0 : r0 + 8, :].astype(f32)
            for c in range(3):
                add = jnp.where(
                    (sub == at_row) & there[d], act * srow_r[e, d, c : c + 1, :], 0.0
                )
                fields[e + 1, c, PAD + r0 : PAD + r0 + 8, :] += add
        for d, (c0, at_lane) in enumerate(((0, 0), (cols - 128, 127))):
            act = act_ref[:, c0 : c0 + 128].astype(f32)
            for c in range(3):
                add = jnp.where(
                    (tile_lane == at_lane) & there[2 + d],
                    act * as_column(scol_r[e, d, c : c + 1, :]),
                    0.0,
                )
                fields[e + 1, c, PAD : PAD + rows, c0 : c0 + 128] += add

    slope_store = pltpu.make_async_copy(
        fields.at[SECTIONS, :, pl.ds(PAD, rows), :], slope_out, loc.at[4]
    )
    slope_store.start()

    for c in range(3):
        pieces = split3(fields[SECTIONS, c, PAD : PAD + rows, :])
        for p in range(3):
            parts[p, :, c * cols : (c + 1) * cols] = pieces[p]

    def pack(j, carry):
        pick = jnp.where(chosen(j), 1.0, 0.0).astype(jnp.bfloat16)
        dst = pl.ds(pl.multiple_of(j * SC, SC), SC)
        for c in range(3):
            w = slice(c * cols, (c + 1) * cols)
            total = jnp.dot(pick, parts[2, :, w], preferred_element_type=f32)
            total += jnp.dot(pick, parts[1, :, w], preferred_element_type=f32)
            total += jnp.dot(pick, parts[0, :, w], preferred_element_type=f32)
            send[dst, w] = total
        return carry

    lax.fori_loop(0, slots // SC, pack, 0)

    def send_blocks(k, carry):
        blk_copy(peer(k), me).start()
        return carry

    lax.fori_loop(1, n, send_blocks, 0)
    own_tags = pltpu.make_async_copy(tag_send.at[at(me), :], tag_recv.at[at(me), :], loc.at[5])
    own_blk = pltpu.make_async_copy(send.at[at(me), :], recv.at[at(me), :], loc.at[6])
    own_tags.start()
    own_blk.start()

    def got_tags(k, carry):
        tag_copy(peer(k), peer(k)).wait_recv()
        return carry

    lax.fori_loop(1, n, got_tags, 0)
    own_tags.wait()
    tag_row = jnp.transpose(tag_recv[...])[0:1, :]

    def land(i, carry):
        want = (lax.broadcasted_iota(jnp.int32, (SC, slots), 0) + (i * SC + 1)).astype(f32)
        hot[pl.ds(pl.multiple_of(i * SC, SC), SC), :] = jnp.where(want == tag_row, 1.0, 0.0).astype(
            jnp.bfloat16
        )
        return carry

    lax.fori_loop(0, lrows // SC, land, 0)
    for c in load_m + [load_h, load_d]:
        c.wait()

    def got_blocks(k, carry):
        blk_copy(peer(k), peer(k)).wait_recv()
        return carry

    lax.fori_loop(1, n, got_blocks, 0)
    own_blk.wait()

    for c in range(3):

        def cut(j, carry):
            here = pl.ds(pl.multiple_of(j * SC, SC), SC)
            for p, piece in enumerate(split3(recv[here, c * cols : (c + 1) * cols])):
                rparts[p, here, :] = piece
            return carry

        lax.fori_loop(0, slots // SC, cut, 0)

        def inflow(i, carry):
            here = pl.ds(pl.multiple_of(i * SC, SC), SC)
            pick = hot[here, :]
            total = jnp.dot(pick, rparts[2], preferred_element_type=f32)
            total += jnp.dot(pick, rparts[1], preferred_element_type=f32)
            total += jnp.dot(pick, rparts[0], preferred_element_type=f32)
            if c == 0:
                lh[here, :] += total
            else:
                vec[0, c - 1, pl.ds(pl.multiple_of(i * SC + PAD, PAD), SC), :] += total
            return carry

        lax.fori_loop(0, lrows // SC, inflow, 0)
        if c == 0:
            height_store = pltpu.make_async_copy(lh, height_out, loc.at[2])
            height_store.start()

    spot = lax.broadcasted_iota(jnp.int32, (1, 128), 1)
    mine = jnp.zeros((1, 128), f32)
    for e in range(3):
        for c in range(2):
            lrow_s[e, 0, c : c + 1, :] = vec[e, c, PAD + lrows - 8 : PAD + lrows, :][7:8, :]
            lrow_s[e, 1, c : c + 1, :] = vec[e, c, PAD : PAD + 8, :][0:1, :]
            lcol_s[e, 0, c : c + 1, :] = column(
                vec[e, c, PAD : PAD + lrows, cols - 128 : cols], 127
            )
            lcol_s[e, 1, c : c + 1, :] = column(vec[e, c, PAD : PAD + lrows, 0:128], 0)
        copies = halo_copies(e, lrow_s, lrow_r, lcol_s, lcol_r, lk_ss, lk_rs)
        for c in copies:
            c.start()
        pending += copies

        def stencil(i, carry):
            base = pl.multiple_of(i * RB, RB)
            here = pl.ds(base, RB)
            diag = (1.0 + 4.0 * dispersion - SHIFT) + ld[here, :]
            result = []
            for c in range(2):
                x = vec[e, c, pl.ds(base, RB + 2 * PAD), :]
                mid = x[PAD : PAD + RB, :]
                beside = x[PAD - 1 : PAD - 1 + RB, :] + x[PAD + 1 : PAD + 1 + RB, :]
                beside = beside + from_left(mid) + from_right(mid)
                image = diag * mid - dispersion * beside
                if e < 2:
                    vec[e + 1, c, pl.ds(pl.multiple_of(base + PAD, PAD), RB), :] = image
                for q, term in enumerate((mid * mid, mid * image)):
                    result.append(
                        carry[2 * c + q] + jnp.sum(term.reshape(RB // 8, 8, cols), axis=0)
                    )
            return tuple(result)

        sums = lax.fori_loop(
            0, lrows // RB, stencil, tuple(jnp.zeros((8, cols), f32) for _ in range(4))
        )
        for c in copies:
            c.wait_recv()
        for c in range(2):
            halo_row = [
                jnp.where(there[d], lrow_r[e, d, c : c + 1, :], 0.0) for d in range(2)
            ]
            halo_col = [
                jnp.where(there[2 + d], lcol_r[e, d, c : c + 1, :], 0.0) for d in range(2)
            ]
            edge_r = lrow_s[e, 1, c : c + 1, :] * halo_row[0] + lrow_s[e, 0, c : c + 1, :] * halo_row[1]
            edge_c = lcol_s[e, 1, c : c + 1, :] * halo_col[0] + lcol_s[e, 0, c : c + 1, :] * halo_col[1]
            even = jnp.sum(sums[2 * c], axis=0, keepdims=True)
            odd = jnp.sum(sums[2 * c + 1], axis=0, keepdims=True) - dispersion * edge_r
            even = jnp.sum(even, axis=1, keepdims=True)
            odd = jnp.sum(odd, axis=1, keepdims=True) - dispersion * jnp.sum(
                edge_c, axis=1, keepdims=True
            )
            mine = jnp.where(spot == 6 * c + 2 * e, even, mine)
            mine = jnp.where(spot == 6 * c + 2 * e + 1, odd, mine)
            if e < 2:
                sub = lax.broadcasted_iota(jnp.int32, (8, cols), 0)
                for d, (r0, at_row) in enumerate(((0, 0), (lrows - 8, 7))):
                    vec[e + 1, c, PAD + r0 : PAD + r0 + 8, :] -= jnp.where(
                        sub == at_row, dispersion * halo_row[d], 0.0
                    )
                tile_lane = lax.broadcasted_iota(jnp.int32, (lrows, 128), 1)
                for d, (c0, at_lane) in enumerate(((0, 0), (cols - 128, 127))):
                    vec[e + 1, c, PAD : PAD + lrows, c0 : c0 + 128] -= jnp.where(
                        tile_lane == at_lane, dispersion * as_column(halo_col[d]), 0.0
                    )

    sum_s[...] = mine

    def sum_copy(t, s):
        return pltpu.make_async_remote_copy(
            src_ref=sum_s,
            dst_ref=sum_r.at[s],
            send_sem=sum_ss.at[t],
            recv_sem=sum_rs.at[s],
            device_id=coords(t),
            device_id_type=MESH,
        )

    def send_sums(k, carry):
        sum_copy(peer(k), me).start()
        return carry

    lax.fori_loop(1, n, send_sums, 0)

    for c in pending:
        c.wait_send()

    def sent(k, carry):
        tag_copy(peer(k), me).wait_send()
        blk_copy(peer(k), me).wait_send()
        return carry

    lax.fori_loop(1, n, sent, 0)

    def got_sums(k, total):
        s = peer(k)
        sum_copy(s, s).wait_recv()
        return total

    lax.fori_loop(1, n, got_sums, 0)
    sum_r[me] = mine
    total = jnp.sum(sum_r[...], axis=0)

    stores = []
    for c in range(2):
        nu = [
            jnp.sum(jnp.where(spot == 6 * c + k, total, 0.0), axis=1, keepdims=True)
            for k in range(6)
        ]
        hk = [nu[k + 1] + SHIFT * nu[k] for k in range(5)]
        l10 = hk[1] / hk[0]
        l20 = hk[2] / hk[0]
        d1 = hk[2] - l10 * hk[1]
        s21 = hk[3] - l20 * hk[1]
        l21 = s21 / d1
        d2 = hk[4] - l20 * hk[2] - l21 * s21
        y1 = nu[1] - l10 * nu[0]
        y2 = nu[2] - l20 * nu[0] - l21 * y1
        c2 = y2 / d2
        c1 = y1 / d1 - l21 * c2
        c0 = nu[0] / hk[0] - l10 * c1 - l20 * c2

        def combine(i, carry):
            here = pl.ds(pl.multiple_of(i * RB + PAD, PAD), RB)
            vec[0, c, here, :] = (
                c0 * vec[0, c, here, :] + c1 * vec[1, c, here, :] + c2 * vec[2, c, here, :]
            )
            return carry

        lax.fori_loop(0, lrows // RB, combine, 0)
        store = pltpu.make_async_copy(
            vec.at[0, c, pl.ds(PAD, lrows), :], lake_out.at[c], loc.at[c]
        )
        store.start()
        stores.append(store)

    def sent_sums(k, carry):
        sum_copy(peer(k), me).wait_send()
        return carry

    lax.fori_loop(1, n, sent_sums, 0)
    slope_store.wait()
    height_store.wait()
    for store in stores:
        store.wait()


def per_device(
    n0,
    n1,
    slope_depth,
    slope_momentum,
    bed_slope,
    friction,
    slope_active,
    owners,
    offsets,
    lake_height,
    lake_momentum,
    lake_diagonal,
):
    n = n0 * n1
    rows, cols = slope_depth.shape
    lrows = lake_height.shape[0]
    cap = -(-max(2, 2 * rows // n) // 8) * 8
    slots = n * cap
    f32 = jnp.float32
    dma = pltpu.SemaphoreType.DMA
    vmem = pl.BlockSpec(memory_space=pltpu.VMEM)
    hbm = pl.BlockSpec(memory_space=pl.ANY)
    return pl.pallas_call(
        functools.partial(kernel, n0, n1, cap),
        out_shape=(
            jax.ShapeDtypeStruct((3, rows, cols), f32),
            jax.ShapeDtypeStruct((lrows, cols), f32),
            jax.ShapeDtypeStruct((2, lrows, cols), f32),
        ),
        in_specs=[vmem] * 8 + [hbm] * 3,
        out_specs=(hbm,) * 3,
        scratch_shapes=[
            pltpu.VMEM((SECTIONS + 1, 3, rows + 2 * PAD, cols), f32),
            pltpu.VMEM((3, rows, 3 * cols), jnp.bfloat16),
            pltpu.VMEM((slots, 3 * cols), f32),
            pltpu.VMEM((slots, 3 * cols), f32),
            pltpu.VMEM((slots, 128), f32),
            pltpu.VMEM((slots, 128), f32),
            pltpu.VMEM((lrows, slots), jnp.bfloat16),
            pltpu.VMEM((3, slots, cols), jnp.bfloat16),
            pltpu.VMEM((3, 2, lrows + 2 * PAD, cols), f32),
            pltpu.VMEM((lrows, cols), f32),
            pltpu.VMEM((lrows, cols), f32),
            pltpu.VMEM((SECTIONS, 2, 3, cols), f32),
            pltpu.VMEM((SECTIONS, 2, 3, cols), f32),
            pltpu.VMEM((SECTIONS, 2, 3, rows), f32),
            pltpu.VMEM((SECTIONS, 2, 3, rows), f32),
            pltpu.VMEM((3, 2, 2, cols), f32),
            pltpu.VMEM((3, 2, 2, cols), f32),
            pltpu.VMEM((3, 2, 2, lrows), f32),
            pltpu.VMEM((3, 2, 2, lrows), f32),
            pltpu.VMEM((1, 128), f32),
            pltpu.VMEM((n, 1, 128), f32),
            dma((n,)),
            dma((n,)),
            dma((n,)),
            dma((n,)),
            dma((SECTIONS, 4)),
            dma((SECTIONS, 4)),
            dma((3, 4)),
            dma((3, 4)),
            dma((n,)),
            dma((n,)),
            dma((7,)),
        ],
        compiler_params=pltpu.CompilerParams(
            collective_id=0, has_side_effects=True, vmem_limit_bytes=58 * 1024 * 1024
        ),
    )(
        slope_depth,
        slope_momentum,
        bed_slope,
        friction,
        slope_active,
        owners.reshape(1, rows),
        owners.reshape(rows, 1),
        offsets.reshape(1, rows),
        lake_height,
        lake_momentum,
        lake_diagonal,
    )


def solution(mesh):
    return jax.shard_map(
        functools.partial(per_device, mesh.shape["gx"], mesh.shape["gy"]),
        mesh=mesh,
        in_specs=(
            P("gx", "gy"),
            P(None, "gx", "gy"),
            P(None, "gx", "gy"),
            P("gx", "gy"),
            P("gx", "gy"),
            P("gx", "gy", None, None),
            P("gx", "gy", None),
            P("gx", "gy"),
            P(None, "gx", "gy"),
            P("gx", "gy"),
        ),
        out_specs=(P(None, "gx", "gy"), P("gx", "gy"), P(None, "gx", "gy")),
        check_vma=False,
    )
```

```python
import functools

import jax
import jax.numpy as jnp
from jax import lax
from jax.experimental import pallas as pl
from jax.experimental.pallas import tpu as pltpu
from jax.sharding import PartitionSpec as P

SECTIONS = 2
courant = 0.15
depth_floor = 0.25
dispersion = 0.5
SHIFT = 4.1
PAD = 8
MESH = pl.DeviceIdType.MESH


def along_terms(h, m, n, sign):
    inv = 1.0 / jnp.maximum(h, depth_floor)
    u = m * inv
    k = sign * 0.5 * courant
    return (0.25 * h + k * m, 0.25 * m + k * (m * u + 0.5 * h * h), 0.25 * n + k * (n * u))


def across_terms(h, m, n, sign):
    inv = 1.0 / jnp.maximum(h, depth_floor)
    v = n * inv
    k = sign * 0.5 * courant
    return (0.25 * h + k * n, 0.25 * m + k * (m * v), 0.25 * n + k * (n * v + 0.5 * h * h))


def split3(x):
    hi = x.astype(jnp.bfloat16)
    rest = x - hi.astype(jnp.float32)
    mid = rest.astype(jnp.bfloat16)
    low = (rest - mid.astype(jnp.float32)).astype(jnp.bfloat16)
    return hi, mid, low


def column(x, lane):
    return jnp.transpose(x)[lane : lane + 1, :]


def as_column(row):
    return jnp.transpose(jnp.broadcast_to(row, (128, row.shape[1])))


def kernel(
    n0,
    n1,
    cap,
    depth_hbm,
    mom_hbm,
    bed_hbm,
    fric_hbm,
    act_hbm,
    own_row_ref,
    off_ref,
    lh_hbm,
    lm_hbm,
    ld_hbm,
    slope_out,
    height_out,
    lake_out,
    fields,
    parts,
    send,
    recv,
    tag_send,
    tag_recv,
    hot,
    rparts,
    bed_ref,
    fric_ref,
    act_ref,
    vec,
    lh,
    ld,
    srow_s,
    srow_r,
    scol_s,
    scol_r,
    lrow_s,
    lrow_r,
    lcol_s,
    lcol_r,
    sum_s,
    sum_r,
    tag_ss,
    tag_rs,
    blk_ss,
    blk_rs,
    sl_ss,
    sl_rs,
    lk_ss,
    lk_rs,
    sum_ss,
    sum_rs,
    loc,
):
    n = n0 * n1
    gx = lax.axis_index("gx")
    gy = lax.axis_index("gy")
    me = gx * n1 + gy
    rows, cols = fric_ref.shape
    lrows = lh.shape[0]
    slots = n * cap
    f32 = jnp.float32

    def peer(k):
        return lax.rem(me + k, n)

    def coords(t):
        return (lax.div(t, n1), lax.rem(t, n1))

    load_f = [
        pltpu.make_async_copy(src, fields.at[0, c, pl.ds(PAD, rows), :], loc.at[7 + c])
        for c, src in enumerate((depth_hbm, mom_hbm.at[0], mom_hbm.at[1]))
    ]
    load_s = [
        pltpu.make_async_copy(bed_hbm, bed_ref, loc.at[10]),
        pltpu.make_async_copy(fric_hbm, fric_ref, loc.at[11]),
        pltpu.make_async_copy(act_hbm, act_ref, loc.at[12]),
    ]
    for c in load_f + load_s:
        c.start()
    load_m = [
        pltpu.make_async_copy(lm_hbm.at[c], vec.at[0, c, pl.ds(PAD, lrows), :], loc.at[c])
        for c in range(2)
    ]
    load_h = pltpu.make_async_copy(lh_hbm, lh, loc.at[2])
    load_d = pltpu.make_async_copy(ld_hbm, ld, loc.at[3])

    barrier = pltpu.get_barrier_semaphore()

    def greet(k, carry):
        pl.semaphore_signal(barrier, inc=1, device_id=coords(peer(k)), device_id_type=MESH)
        return carry

    lax.fori_loop(1, n, greet, 0)

    own_row = own_row_ref[...]
    own_real = own_row.astype(f32)
    own_col = as_column(own_real)[:, 0:1]
    before = lax.broadcasted_iota(jnp.int32, (rows, rows), 0) < lax.broadcasted_iota(
        jnp.int32, (rows, rows), 1
    )
    rank = jnp.sum(
        jnp.where((own_col == own_real) & before, 1.0, 0.0), axis=0, keepdims=True
    )
    slot = lax.rem(own_row - me + n, n) * cap + rank.astype(jnp.int32)
    off = (off_ref[...] + 1).astype(f32)
    SC = 128

    def chosen(j):
        return (lax.broadcasted_iota(jnp.int32, (SC, rows), 0) + j * SC) == slot

    def tags(j, carry):
        col = jnp.sum(jnp.where(chosen(j), off, 0.0), axis=1, keepdims=True)
        tag_send[pl.ds(pl.multiple_of(j * SC, SC), SC), :] = jnp.broadcast_to(col, (SC, 128))
        return carry

    lax.fori_loop(0, slots // SC, tags, 0)

    for c in range(3):
        for e in range(SECTIONS):
            fields[e, c, 0:PAD, :] = jnp.zeros((PAD, cols), f32)
            fields[e, c, PAD + rows : PAD + rows + PAD, :] = jnp.zeros((PAD, cols), f32)
    for c in range(2):
        for e in range(3):
            vec[e, c, 0:PAD, :] = jnp.zeros((PAD, cols), f32)
            vec[e, c, PAD + lrows : PAD + lrows + PAD, :] = jnp.zeros((PAD, cols), f32)
    for c in load_m + [load_h, load_d]:
        c.start()
    for c in load_f:
        c.wait()

    def at(k):
        return pl.ds(pl.multiple_of(k * cap, cap), cap)

    def tag_copy(k):
        return pltpu.make_async_remote_copy(
            src_ref=tag_send.at[at(k), :],
            dst_ref=tag_recv.at[at(k), :],
            send_sem=tag_ss.at[k],
            recv_sem=tag_rs.at[k],
            device_id=coords(peer(k)),
            device_id_type=MESH,
        )

    def blk_copy(k):
        return pltpu.make_async_remote_copy(
            src_ref=send.at[at(k), :],
            dst_ref=recv.at[at(k), :],
            send_sem=blk_ss.at[k],
            recv_sem=blk_rs.at[k],
            device_id=coords(peer(k)),
            device_id_type=MESH,
        )

    neighbours = (
        (lax.rem(gx + 1, n0), gy),
        (lax.rem(gx + n0 - 1, n0), gy),
        (gx, lax.rem(gy + 1, n1)),
        (gx, lax.rem(gy + n1 - 1, n1)),
    )
    there = (gx > 0, gx < n0 - 1, gy > 0, gy < n1 - 1)

    def halo_copies(e, row_s, row_r, col_s, col_r, ss, rs):
        out = []
        for d in range(4):
            s, r = (row_s, row_r) if d < 2 else (col_s, col_r)
            out.append(
                pltpu.make_async_remote_copy(
                    src_ref=s.at[e, d % 2],
                    dst_ref=r.at[e, d % 2],
                    send_sem=ss.at[e, d],
                    recv_sem=rs.at[e, d],
                    device_id=neighbours[d],
                    device_id_type=MESH,
                )
            )
        return out

    pending = []
    RB = 64
    lane = lax.broadcasted_iota(jnp.int32, (RB, cols), 1)
    first_lane = lane == 0
    last_lane = lane == cols - 1

    def from_left(x):
        return jnp.where(first_lane, 0.0, pltpu.roll(x, 1, 1))

    def from_right(x):
        return jnp.where(last_lane, 0.0, pltpu.roll(x, cols - 1, 1))

    for e in range(SECTIONS):
        lo = [fields[e, c, PAD : PAD + 8, :] for c in range(3)]
        hi = [fields[e, c, PAD + rows - 8 : PAD + rows, :] for c in range(3)]
        for c, x in enumerate(along_terms(*hi, 1.0)):
            srow_s[e, 0, c : c + 1, :] = x[7:8, :]
        for c, x in enumerate(along_terms(*lo, -1.0)):
            srow_s[e, 1, c : c + 1, :] = x[0:1, :]
        right = [fields[e, c, PAD : PAD + rows, cols - 128 : cols] for c in range(3)]
        for c, x in enumerate(across_terms(*right, 1.0)):
            scol_s[e, 0, c : c + 1, :] = column(x, 127)
        left = [fields[e, c, PAD : PAD + rows, 0:128] for c in range(3)]
        for c, x in enumerate(across_terms(*left, -1.0)):
            scol_s[e, 1, c : c + 1, :] = column(x, 0)
        copies = halo_copies(e, srow_s, srow_r, scol_s, scol_r, sl_ss, sl_rs)
        if e == 0:
            pl.semaphore_wait(barrier, n - 1)
        for c in copies:
            c.start()
        pending += copies
        if e == 0:

            def send_tags(k, carry):
                tag_copy(k).start()
                return carry

            lax.fori_loop(1, n, send_tags, 0)
            for c in load_s:
                c.wait()

        def section(i, carry):
            base = pl.multiple_of(i * RB, RB)
            x = [fields[e, c, pl.ds(base, RB + 2 * PAD), :] for c in range(3)]
            mid = [v[PAD : PAD + RB, :] for v in x]
            below = along_terms(*[v[PAD - 1 : PAD - 1 + RB, :] for v in x], 1.0)
            above = along_terms(*[v[PAD + 1 : PAD + 1 + RB, :] for v in x], -1.0)
            left = across_terms(*mid, 1.0)
            right = across_terms(*mid, -1.0)
            here = pl.ds(base, RB)
            active = act_ref[here, :].astype(f32)
            fric = fric_ref[here, :]
            for c in range(3):
                total = below[c] + above[c] + from_left(left[c]) + from_right(right[c])
                if c > 0:
                    total = total + courant * (mid[0] * bed_ref[c - 1, here, :] - fric * mid[c])
                fields[e + 1, c, pl.ds(pl.multiple_of(base + PAD, PAD), RB), :] = total * active
            return carry

        lax.fori_loop(0, rows // RB, section, 0)
        for c in copies:
            c.wait_recv()
        sub = lax.broadcasted_iota(jnp.int32, (8, cols), 0)
        tile_lane = lax.broadcasted_iota(jnp.int32, (rows, 128), 1)
        for d, (r0, at_row) in enumerate(((0, 0), (rows - 8, 7))):
            act = act_ref[r0 : r0 + 8, :].astype(f32)
            for c in range(3):
                add = jnp.where(
                    (sub == at_row) & there[d], act * srow_r[e, d, c : c + 1, :], 0.0
                )
                fields[e + 1, c, PAD + r0 : PAD + r0 + 8, :] += add
        for d, (c0, at_lane) in enumerate(((0, 0), (cols - 128, 127))):
            act = act_ref[:, c0 : c0 + 128].astype(f32)
            for c in range(3):
                add = jnp.where(
                    (tile_lane == at_lane) & there[2 + d],
                    act * as_column(scol_r[e, d, c : c + 1, :]),
                    0.0,
                )
                fields[e + 1, c, PAD : PAD + rows, c0 : c0 + 128] += add

    slope_store = pltpu.make_async_copy(
        fields.at[SECTIONS, :, pl.ds(PAD, rows), :], slope_out, loc.at[4]
    )
    slope_store.start()

    for c in range(3):
        pieces = split3(fields[SECTIONS, c, PAD : PAD + rows, :])
        for p in range(3):
            parts[p, :, c * cols : (c + 1) * cols] = pieces[p]

    per = SC // cap

    def send_block(k, carry):
        blk_copy(k).start()
        return carry

    def pack(j, carry):
        pick = jnp.where(chosen(j), 1.0, 0.0).astype(jnp.bfloat16)
        dst = pl.ds(pl.multiple_of(j * SC, SC), SC)
        for c in range(3):
            w = slice(c * cols, (c + 1) * cols)
            total = jnp.dot(pick, parts[2, :, w], preferred_element_type=f32)
            total += jnp.dot(pick, parts[1, :, w], preferred_element_type=f32)
            total += jnp.dot(pick, parts[0, :, w], preferred_element_type=f32)
            send[dst, w] = total
        lax.fori_loop(lax.max(j * per, 1), (j + 1) * per, send_block, 0)
        return carry

    lax.fori_loop(0, slots // SC, pack, 0)

    own_tags = pltpu.make_async_copy(tag_send.at[at(0), :], tag_recv.at[at(0), :], loc.at[5])
    own_blk = pltpu.make_async_copy(send.at[at(0), :], recv.at[at(0), :], loc.at[6])
    own_tags.start()
    own_blk.start()

    def got_tags(k, carry):
        tag_copy(k).wait_recv()
        return carry

    lax.fori_loop(1, n, got_tags, 0)
    own_tags.wait()
    tag_row = jnp.transpose(tag_recv[...])[0:1, :]

    def land(i, carry):
        want = (lax.broadcasted_iota(jnp.int32, (SC, slots), 0) + (i * SC + 1)).astype(f32)
        pick = jnp.where(want == tag_row, 1.0, 0.0).astype(jnp.bfloat16)
        for q in range(slots // SC):
            hot[q, pl.ds(pl.multiple_of(i * SC, SC), SC), :] = pick[:, q * SC : (q + 1) * SC]
        return carry

    lax.fori_loop(0, lrows // SC, land, 0)
    for c in load_m + [load_h, load_d]:
        c.wait()

    own_blk.wait()

    def got_block(k, carry):
        blk_copy(k).wait_recv()
        return carry

    def arrive(q, carry):
        lax.fori_loop(lax.max(q * per, 1), (q + 1) * per, got_block, 0)
        for c in range(3):
            w = slice(c * cols, (c + 1) * cols)
            pieces = split3(recv[pl.ds(pl.multiple_of(q * SC, SC), SC), w])
            for p in range(3):
                rparts[p, :, w] = pieces[p]

        def inflow(i, inner):
            here = pl.ds(pl.multiple_of(i * SC, SC), SC)
            pick = hot[q, here, :]
            for c in range(3):
                w = slice(c * cols, (c + 1) * cols)
                total = jnp.dot(pick, rparts[2, :, w], preferred_element_type=f32)
                total += jnp.dot(pick, rparts[1, :, w], preferred_element_type=f32)
                total += jnp.dot(pick, rparts[0, :, w], preferred_element_type=f32)
                if c == 0:
                    lh[here, :] += total
                else:
                    vec[0, c - 1, pl.ds(pl.multiple_of(i * SC + PAD, PAD), SC), :] += total
            return inner

        lax.fori_loop(0, lrows // SC, inflow, 0)
        return carry

    lax.fori_loop(0, slots // SC, arrive, 0)
    height_store = pltpu.make_async_copy(lh, height_out, loc.at[2])
    height_store.start()

    spot = lax.broadcasted_iota(jnp.int32, (1, 128), 1)
    mine = jnp.zeros((1, 128), f32)
    for e in range(3):
        for c in range(2):
            lrow_s[e, 0, c : c + 1, :] = vec[e, c, PAD + lrows - 8 : PAD + lrows, :][7:8, :]
            lrow_s[e, 1, c : c + 1, :] = vec[e, c, PAD : PAD + 8, :][0:1, :]
            lcol_s[e, 0, c : c + 1, :] = column(
                vec[e, c, PAD : PAD + lrows, cols - 128 : cols], 127
            )
            lcol_s[e, 1, c : c + 1, :] = column(vec[e, c, PAD : PAD + lrows, 0:128], 0)
        copies = halo_copies(e, lrow_s, lrow_r, lcol_s, lcol_r, lk_ss, lk_rs)
        for c in copies:
            c.start()
        pending += copies

        def stencil(i, carry):
            base = pl.multiple_of(i * RB, RB)
            here = pl.ds(base, RB)
            diag = (1.0 + 4.0 * dispersion - SHIFT) + ld[here, :]
            result = []
            for c in range(2):
                x = vec[e, c, pl.ds(base, RB + 2 * PAD), :]
                mid = x[PAD : PAD + RB, :]
                beside = x[PAD - 1 : PAD - 1 + RB, :] + x[PAD + 1 : PAD + 1 + RB, :]
                beside = beside + from_left(mid) + from_right(mid)
                image = diag * mid - dispersion * beside
                if e < 2:
                    vec[e + 1, c, pl.ds(pl.multiple_of(base + PAD, PAD), RB), :] = image
                for q, term in enumerate((mid * mid, mid * image)):
                    result.append(
                        carry[2 * c + q] + jnp.sum(term.reshape(RB // 8, 8, cols), axis=0)
                    )
            return tuple(result)

        sums = lax.fori_loop(
            0, lrows // RB, stencil, tuple(jnp.zeros((8, cols), f32) for _ in range(4))
        )
        for c in copies:
            c.wait_recv()
        for c in range(2):
            halo_row = [
                jnp.where(there[d], lrow_r[e, d, c : c + 1, :], 0.0) for d in range(2)
            ]
            halo_col = [
                jnp.where(there[2 + d], lcol_r[e, d, c : c + 1, :], 0.0) for d in range(2)
            ]
            edge_r = lrow_s[e, 1, c : c + 1, :] * halo_row[0] + lrow_s[e, 0, c : c + 1, :] * halo_row[1]
            edge_c = lcol_s[e, 1, c : c + 1, :] * halo_col[0] + lcol_s[e, 0, c : c + 1, :] * halo_col[1]
            even = jnp.sum(sums[2 * c], axis=0, keepdims=True)
            odd = jnp.sum(sums[2 * c + 1], axis=0, keepdims=True) - dispersion * edge_r
            even = jnp.sum(even, axis=1, keepdims=True)
            odd = jnp.sum(odd, axis=1, keepdims=True) - dispersion * jnp.sum(
                edge_c, axis=1, keepdims=True
            )
            mine = jnp.where(spot == 6 * c + 2 * e, even, mine)
            mine = jnp.where(spot == 6 * c + 2 * e + 1, odd, mine)
            if e < 2:
                sub = lax.broadcasted_iota(jnp.int32, (8, cols), 0)
                for d, (r0, at_row) in enumerate(((0, 0), (lrows - 8, 7))):
                    vec[e + 1, c, PAD + r0 : PAD + r0 + 8, :] -= jnp.where(
                        sub == at_row, dispersion * halo_row[d], 0.0
                    )
                tile_lane = lax.broadcasted_iota(jnp.int32, (lrows, 128), 1)
                for d, (c0, at_lane) in enumerate(((0, 0), (cols - 128, 127))):
                    vec[e + 1, c, PAD : PAD + lrows, c0 : c0 + 128] -= jnp.where(
                        tile_lane == at_lane, dispersion * as_column(halo_col[d]), 0.0
                    )

    sum_s[...] = mine

    def sum_copy(t, s):
        return pltpu.make_async_remote_copy(
            src_ref=sum_s,
            dst_ref=sum_r.at[s],
            send_sem=sum_ss.at[t],
            recv_sem=sum_rs.at[s],
            device_id=coords(t),
            device_id_type=MESH,
        )

    def send_sums(k, carry):
        sum_copy(peer(k), me).start()
        return carry

    lax.fori_loop(1, n, send_sums, 0)

    for c in pending:
        c.wait_send()

    def sent(k, carry):
        tag_copy(k).wait_send()
        blk_copy(k).wait_send()
        return carry

    lax.fori_loop(1, n, sent, 0)

    def got_sums(k, total):
        s = peer(k)
        sum_copy(s, s).wait_recv()
        return total

    lax.fori_loop(1, n, got_sums, 0)
    sum_r[me] = mine
    total = jnp.sum(sum_r[...], axis=0)

    stores = []
    for c in range(2):
        nu = [
            jnp.sum(jnp.where(spot == 6 * c + k, total, 0.0), axis=1, keepdims=True)
            for k in range(6)
        ]
        hk = [nu[k + 1] + SHIFT * nu[k] for k in range(5)]
        l10 = hk[1] / hk[0]
        l20 = hk[2] / hk[0]
        d1 = hk[2] - l10 * hk[1]
        s21 = hk[3] - l20 * hk[1]
        l21 = s21 / d1
        d2 = hk[4] - l20 * hk[2] - l21 * s21
        y1 = nu[1] - l10 * nu[0]
        y2 = nu[2] - l20 * nu[0] - l21 * y1
        c2 = y2 / d2
        c1 = y1 / d1 - l21 * c2
        c0 = nu[0] / hk[0] - l10 * c1 - l20 * c2

        def combine(i, carry):
            here = pl.ds(pl.multiple_of(i * RB + PAD, PAD), RB)
            vec[0, c, here, :] = (
                c0 * vec[0, c, here, :] + c1 * vec[1, c, here, :] + c2 * vec[2, c, here, :]
            )
            return carry

        lax.fori_loop(0, lrows // RB, combine, 0)
        store = pltpu.make_async_copy(
            vec.at[0, c, pl.ds(PAD, lrows), :], lake_out.at[c], loc.at[c]
        )
        store.start()
        stores.append(store)

    def sent_sums(k, carry):
        sum_copy(peer(k), me).wait_send()
        return carry

    lax.fori_loop(1, n, sent_sums, 0)
    slope_store.wait()
    height_store.wait()
    for store in stores:
        store.wait()


def per_device(
    n0,
    n1,
    slope_depth,
    slope_momentum,
    bed_slope,
    friction,
    slope_active,
    owners,
    offsets,
    lake_height,
    lake_momentum,
    lake_diagonal,
):
    n = n0 * n1
    rows, cols = slope_depth.shape
    lrows = lake_height.shape[0]
    cap = -(-max(2, 2 * rows // n) // 8) * 8
    slots = n * cap
    f32 = jnp.float32
    dma = pltpu.SemaphoreType.DMA
    vmem = pl.BlockSpec(memory_space=pltpu.VMEM)
    hbm = pl.BlockSpec(memory_space=pl.ANY)
    return pl.pallas_call(
        functools.partial(kernel, n0, n1, cap),
        out_shape=(
            jax.ShapeDtypeStruct((3, rows, cols), f32),
            jax.ShapeDtypeStruct((lrows, cols), f32),
            jax.ShapeDtypeStruct((2, lrows, cols), f32),
        ),
        in_specs=[hbm] * 5 + [vmem] * 2 + [hbm] * 3,
        out_specs=(hbm,) * 3,
        scratch_shapes=[
            pltpu.VMEM((SECTIONS + 1, 3, rows + 2 * PAD, cols), f32),
            pltpu.VMEM((3, rows, 3 * cols), jnp.bfloat16),
            pltpu.VMEM((slots, 3 * cols), f32),
            pltpu.VMEM((slots, 3 * cols), f32),
            pltpu.VMEM((slots, 128), f32),
            pltpu.VMEM((slots, 128), f32),
            pltpu.VMEM((slots // 128, lrows, 128), jnp.bfloat16),
            pltpu.VMEM((3, 128, 3 * cols), jnp.bfloat16),
            pltpu.VMEM((2, rows, cols), f32),
            pltpu.VMEM((rows, cols), f32),
            pltpu.VMEM((rows, cols), slope_active.dtype),
            pltpu.VMEM((3, 2, lrows + 2 * PAD, cols), f32),
            pltpu.VMEM((lrows, cols), f32),
            pltpu.VMEM((lrows, cols), f32),
            pltpu.VMEM((SECTIONS, 2, 3, cols), f32),
            pltpu.VMEM((SECTIONS, 2, 3, cols), f32),
            pltpu.VMEM((SECTIONS, 2, 3, rows), f32),
            pltpu.VMEM((SECTIONS, 2, 3, rows), f32),
            pltpu.VMEM((3, 2, 2, cols), f32),
            pltpu.VMEM((3, 2, 2, cols), f32),
            pltpu.VMEM((3, 2, 2, lrows), f32),
            pltpu.VMEM((3, 2, 2, lrows), f32),
            pltpu.VMEM((1, 128), f32),
            pltpu.VMEM((n, 1, 128), f32),
            dma((n,)),
            dma((n,)),
            dma((n,)),
            dma((n,)),
            dma((SECTIONS, 4)),
            dma((SECTIONS, 4)),
            dma((3, 4)),
            dma((3, 4)),
            dma((n,)),
            dma((n,)),
            dma((13,)),
        ],
        compiler_params=pltpu.CompilerParams(
            collective_id=0, has_side_effects=True, vmem_limit_bytes=58 * 1024 * 1024
        ),
    )(
        slope_depth,
        slope_momentum,
        bed_slope,
        friction,
        slope_active,
        owners.reshape(1, rows),
        offsets.reshape(1, rows),
        lake_height,
        lake_momentum,
        lake_diagonal,
    )


def solution(mesh):
    return jax.shard_map(
        functools.partial(per_device, mesh.shape["gx"], mesh.shape["gy"]),
        mesh=mesh,
        in_specs=(
            P("gx", "gy"),
            P(None, "gx", "gy"),
            P(None, "gx", "gy"),
            P("gx", "gy"),
            P("gx", "gy"),
            P("gx", "gy", None, None),
            P("gx", "gy", None),
            P("gx", "gy"),
            P(None, "gx", "gy"),
            P("gx", "gy"),
        ),
        out_specs=(P(None, "gx", "gy"), P("gx", "gy"), P(None, "gx", "gy")),
        check_vma=False,
    )
```

```python
import functools

import jax
import jax.numpy as jnp
from jax import lax
from jax.experimental import pallas as pl
from jax.experimental.pallas import tpu as pltpu
from jax.sharding import PartitionSpec as P

SECTIONS = 2
courant = 0.15
depth_floor = 0.25
dispersion = 0.5
SHIFT = 4.1
PAD = 8
MESH = pl.DeviceIdType.MESH


def along_terms(h, m, n, sign):
    inv = 1.0 / jnp.maximum(h, depth_floor)
    u = m * inv
    k = sign * 0.5 * courant
    return (0.25 * h + k * m, 0.25 * m + k * (m * u + 0.5 * h * h), 0.25 * n + k * (n * u))


def across_terms(h, m, n, sign):
    inv = 1.0 / jnp.maximum(h, depth_floor)
    v = n * inv
    k = sign * 0.5 * courant
    return (0.25 * h + k * n, 0.25 * m + k * (m * v), 0.25 * n + k * (n * v + 0.5 * h * h))


def split3(x):
    hi = x.astype(jnp.bfloat16)
    rest = x - hi.astype(jnp.float32)
    mid = rest.astype(jnp.bfloat16)
    low = (rest - mid.astype(jnp.float32)).astype(jnp.bfloat16)
    return hi, mid, low


def column(x, lane):
    return jnp.transpose(x)[lane : lane + 1, :]


def as_column(row):
    return jnp.transpose(jnp.broadcast_to(row, (128, row.shape[1])))


def kernel(
    n0,
    n1,
    cap,
    depth_hbm,
    mom_hbm,
    bed_hbm,
    fric_hbm,
    act_hbm,
    own_row_ref,
    off_ref,
    lh_hbm,
    lm_hbm,
    ld_hbm,
    slope_out,
    height_out,
    lake_out,
    fields,
    parts,
    send,
    recv,
    tag_send,
    tag_recv,
    hot,
    rparts,
    bed_ref,
    fric_ref,
    act_ref,
    vec,
    lh,
    ld,
    srow_s,
    srow_r,
    scol_s,
    scol_r,
    lrow_s,
    lrow_r,
    lcol_s,
    lcol_r,
    sum_s,
    sum_r,
    tag_ss,
    tag_rs,
    blk_ss,
    blk_rs,
    sl_ss,
    sl_rs,
    lk_ss,
    lk_rs,
    sum_ss,
    sum_rs,
    loc,
):
    n = n0 * n1
    gx = lax.axis_index("gx")
    gy = lax.axis_index("gy")
    me = gx * n1 + gy
    rows, cols = fric_ref.shape
    lrows = lh.shape[0]
    slots = n * cap
    f32 = jnp.float32

    def peer(k):
        return lax.rem(me + k, n)

    def coords(t):
        return (lax.div(t, n1), lax.rem(t, n1))

    load_f = [
        pltpu.make_async_copy(src, fields.at[0, c, pl.ds(PAD, rows), :], loc.at[7 + c])
        for c, src in enumerate((depth_hbm, mom_hbm.at[0], mom_hbm.at[1]))
    ]
    load_s = [
        pltpu.make_async_copy(bed_hbm, bed_ref, loc.at[10]),
        pltpu.make_async_copy(fric_hbm, fric_ref, loc.at[11]),
        pltpu.make_async_copy(act_hbm, act_ref, loc.at[12]),
    ]
    for c in load_f + load_s:
        c.start()
    load_m = [
        pltpu.make_async_copy(lm_hbm.at[c], vec.at[0, c, pl.ds(PAD, lrows), :], loc.at[c])
        for c in range(2)
    ]
    load_h = pltpu.make_async_copy(lh_hbm, lh, loc.at[2])
    load_d = pltpu.make_async_copy(ld_hbm, ld, loc.at[3])

    barrier = pltpu.get_barrier_semaphore()

    def greet(k, carry):
        pl.semaphore_signal(barrier, inc=1, device_id=coords(peer(k)), device_id_type=MESH)
        return carry

    lax.fori_loop(1, n, greet, 0)

    own_row = own_row_ref[...]
    own_real = own_row.astype(f32)
    own_col = as_column(own_real)[:, 0:1]
    before = lax.broadcasted_iota(jnp.int32, (rows, rows), 0) < lax.broadcasted_iota(
        jnp.int32, (rows, rows), 1
    )
    rank = jnp.sum(
        jnp.where((own_col == own_real) & before, 1.0, 0.0), axis=0, keepdims=True
    )
    slot = lax.rem(own_row - me + n, n) * cap + rank.astype(jnp.int32)
    off = (off_ref[...] + 1).astype(f32)
    SC = 128

    def chosen(j):
        return (lax.broadcasted_iota(jnp.int32, (SC, rows), 0) + j * SC) == slot

    def tags(j, carry):
        col = jnp.sum(jnp.where(chosen(j), off, 0.0), axis=1, keepdims=True)
        tag_send[pl.ds(pl.multiple_of(j * SC, SC), SC), :] = jnp.broadcast_to(col, (SC, 128))
        return carry

    lax.fori_loop(0, slots // SC, tags, 0)

    for c in range(3):
        for e in range(SECTIONS):
            fields[e, c, 0:PAD, :] = jnp.zeros((PAD, cols), f32)
            fields[e, c, PAD + rows : PAD + rows + PAD, :] = jnp.zeros((PAD, cols), f32)
    for c in range(2):
        for e in range(3):
            vec[e, c, 0:PAD, :] = jnp.zeros((PAD, cols), f32)
            vec[e, c, PAD + lrows : PAD + lrows + PAD, :] = jnp.zeros((PAD, cols), f32)
    for c in load_m + [load_h, load_d]:
        c.start()
    for c in load_f:
        c.wait()

    def at(k):
        return pl.ds(pl.multiple_of(k * cap, cap), cap)

    def tag_copy(k):
        return pltpu.make_async_remote_copy(
            src_ref=tag_send.at[at(k), :],
            dst_ref=tag_recv.at[at(k), :],
            send_sem=tag_ss.at[k],
            recv_sem=tag_rs.at[k],
            device_id=coords(peer(k)),
            device_id_type=MESH,
        )

    def blk_copy(k):
        return pltpu.make_async_remote_copy(
            src_ref=send.at[at(k), :],
            dst_ref=recv.at[at(k), :],
            send_sem=blk_ss.at[k],
            recv_sem=blk_rs.at[k],
            device_id=coords(peer(k)),
            device_id_type=MESH,
        )

    neighbours = (
        (lax.rem(gx + 1, n0), gy),
        (lax.rem(gx + n0 - 1, n0), gy),
        (gx, lax.rem(gy + 1, n1)),
        (gx, lax.rem(gy + n1 - 1, n1)),
    )
    there = (gx > 0, gx < n0 - 1, gy > 0, gy < n1 - 1)

    def halo_copies(e, row_s, row_r, col_s, col_r, ss, rs):
        out = []
        for d in range(4):
            s, r = (row_s, row_r) if d < 2 else (col_s, col_r)
            out.append(
                pltpu.make_async_remote_copy(
                    src_ref=s.at[e, d % 2],
                    dst_ref=r.at[e, d % 2],
                    send_sem=ss.at[e, d],
                    recv_sem=rs.at[e, d],
                    device_id=neighbours[d],
                    device_id_type=MESH,
                )
            )
        return out

    pending = []
    RB = 16
    lane = lax.broadcasted_iota(jnp.int32, (RB, cols), 1)
    first_lane = lane == 0
    last_lane = lane == cols - 1

    def from_left(x):
        return jnp.where(first_lane, 0.0, pltpu.roll(x, 1, 1))

    def from_right(x):
        return jnp.where(last_lane, 0.0, pltpu.roll(x, cols - 1, 1))

    for e in range(SECTIONS):
        lo = [fields[e, c, PAD : PAD + 8, :] for c in range(3)]
        hi = [fields[e, c, PAD + rows - 8 : PAD + rows, :] for c in range(3)]
        for c, x in enumerate(along_terms(*hi, 1.0)):
            srow_s[e, 0, c : c + 1, :] = x[7:8, :]
        for c, x in enumerate(along_terms(*lo, -1.0)):
            srow_s[e, 1, c : c + 1, :] = x[0:1, :]
        right = [fields[e, c, PAD : PAD + rows, cols - 128 : cols] for c in range(3)]
        for c, x in enumerate(across_terms(*right, 1.0)):
            scol_s[e, 0, c : c + 1, :] = column(x, 127)
        left = [fields[e, c, PAD : PAD + rows, 0:128] for c in range(3)]
        for c, x in enumerate(across_terms(*left, -1.0)):
            scol_s[e, 1, c : c + 1, :] = column(x, 0)
        copies = halo_copies(e, srow_s, srow_r, scol_s, scol_r, sl_ss, sl_rs)
        if e == 0:
            pl.semaphore_wait(barrier, n - 1)
        for c in copies:
            c.start()
        pending += copies
        if e == 0:

            def send_tags(k, carry):
                tag_copy(k).start()
                return carry

            lax.fori_loop(1, n, send_tags, 0)
            for c in load_s:
                c.wait()

        def section(i, carry):
            base = pl.multiple_of(i * RB, RB)
            x = [fields[e, c, pl.ds(base, RB + 2 * PAD), :] for c in range(3)]
            mid = [v[PAD : PAD + RB, :] for v in x]
            below = along_terms(*[v[PAD - 1 : PAD - 1 + RB, :] for v in x], 1.0)
            above = along_terms(*[v[PAD + 1 : PAD + 1 + RB, :] for v in x], -1.0)
            left = across_terms(*mid, 1.0)
            right = across_terms(*mid, -1.0)
            here = pl.ds(base, RB)
            active = act_ref[here, :].astype(f32)
            fric = fric_ref[here, :]
            for c in range(3):
                total = below[c] + above[c] + from_left(left[c]) + from_right(right[c])
                if c > 0:
                    total = total + courant * (mid[0] * bed_ref[c - 1, here, :] - fric * mid[c])
                fields[e + 1, c, pl.ds(pl.multiple_of(base + PAD, PAD), RB), :] = total * active
            return carry

        lax.fori_loop(0, rows // RB, section, 0)
        for c in copies:
            c.wait_recv()
        sub = lax.broadcasted_iota(jnp.int32, (8, cols), 0)
        tile_lane = lax.broadcasted_iota(jnp.int32, (rows, 128), 1)
        for d, (r0, at_row) in enumerate(((0, 0), (rows - 8, 7))):
            act = act_ref[r0 : r0 + 8, :].astype(f32)
            for c in range(3):
                add = jnp.where(
                    (sub == at_row) & there[d], act * srow_r[e, d, c : c + 1, :], 0.0
                )
                fields[e + 1, c, PAD + r0 : PAD + r0 + 8, :] += add
        for d, (c0, at_lane) in enumerate(((0, 0), (cols - 128, 127))):
            act = act_ref[:, c0 : c0 + 128].astype(f32)
            for c in range(3):
                add = jnp.where(
                    (tile_lane == at_lane) & there[2 + d],
                    act * as_column(scol_r[e, d, c : c + 1, :]),
                    0.0,
                )
                fields[e + 1, c, PAD : PAD + rows, c0 : c0 + 128] += add

    slope_store = pltpu.make_async_copy(
        fields.at[SECTIONS, :, pl.ds(PAD, rows), :], slope_out, loc.at[4]
    )
    slope_store.start()

    for c in range(3):
        pieces = split3(fields[SECTIONS, c, PAD : PAD + rows, :])
        for p in range(3):
            parts[p, :, c * cols : (c + 1) * cols] = pieces[p]

    per = SC // cap

    def send_block(k, carry):
        blk_copy(k).start()
        return carry

    def pack(j, carry):
        pick = jnp.where(chosen(j), 1.0, 0.0).astype(jnp.bfloat16)
        dst = pl.ds(pl.multiple_of(j * SC, SC), SC)
        for c in range(3):
            w = slice(c * cols, (c + 1) * cols)
            total = jnp.dot(pick, parts[2, :, w], preferred_element_type=f32)
            total += jnp.dot(pick, parts[1, :, w], preferred_element_type=f32)
            total += jnp.dot(pick, parts[0, :, w], preferred_element_type=f32)
            send[dst, w] = total
        lax.fori_loop(lax.max(j * per, 1), (j + 1) * per, send_block, 0)
        return carry

    lax.fori_loop(0, slots // SC, pack, 0)

    own_tags = pltpu.make_async_copy(tag_send.at[at(0), :], tag_recv.at[at(0), :], loc.at[5])
    own_blk = pltpu.make_async_copy(send.at[at(0), :], recv.at[at(0), :], loc.at[6])
    own_tags.start()
    own_blk.start()

    def got_tags(k, carry):
        tag_copy(k).wait_recv()
        return carry

    lax.fori_loop(1, n, got_tags, 0)
    own_tags.wait()
    tag_row = jnp.transpose(tag_recv[...])[0:1, :]

    def land(i, carry):
        want = (lax.broadcasted_iota(jnp.int32, (SC, slots), 0) + (i * SC + 1)).astype(f32)
        pick = jnp.where(want == tag_row, 1.0, 0.0).astype(jnp.bfloat16)
        for q in range(slots // SC):
            hot[q, pl.ds(pl.multiple_of(i * SC, SC), SC), :] = pick[:, q * SC : (q + 1) * SC]
        return carry

    lax.fori_loop(0, lrows // SC, land, 0)
    for c in load_m + [load_h, load_d]:
        c.wait()

    own_blk.wait()

    def got_block(k, carry):
        blk_copy(k).wait_recv()
        return carry

    def arrive(q, carry):
        lax.fori_loop(lax.max(q * per, 1), (q + 1) * per, got_block, 0)
        for c in range(3):
            w = slice(c * cols, (c + 1) * cols)
            pieces = split3(recv[pl.ds(pl.multiple_of(q * SC, SC), SC), w])
            for p in range(3):
                rparts[p, :, w] = pieces[p]

        def inflow(i, inner):
            here = pl.ds(pl.multiple_of(i * SC, SC), SC)
            pick = hot[q, here, :]
            for c in range(3):
                w = slice(c * cols, (c + 1) * cols)
                total = jnp.dot(pick, rparts[2, :, w], preferred_element_type=f32)
                total += jnp.dot(pick, rparts[1, :, w], preferred_element_type=f32)
                total += jnp.dot(pick, rparts[0, :, w], preferred_element_type=f32)
                if c == 0:
                    lh[here, :] += total
                else:
                    vec[0, c - 1, pl.ds(pl.multiple_of(i * SC + PAD, PAD), SC), :] += total
            return inner

        lax.fori_loop(0, lrows // SC, inflow, 0)
        return carry

    lax.fori_loop(0, slots // SC, arrive, 0)
    height_store = pltpu.make_async_copy(lh, height_out, loc.at[2])
    height_store.start()

    spot = lax.broadcasted_iota(jnp.int32, (1, 128), 1)
    mine = jnp.zeros((1, 128), f32)
    for e in range(3):
        for c in range(2):
            lrow_s[e, 0, c : c + 1, :] = vec[e, c, PAD + lrows - 8 : PAD + lrows, :][7:8, :]
            lrow_s[e, 1, c : c + 1, :] = vec[e, c, PAD : PAD + 8, :][0:1, :]
            lcol_s[e, 0, c : c + 1, :] = column(
                vec[e, c, PAD : PAD + lrows, cols - 128 : cols], 127
            )
            lcol_s[e, 1, c : c + 1, :] = column(vec[e, c, PAD : PAD + lrows, 0:128], 0)
        copies = halo_copies(e, lrow_s, lrow_r, lcol_s, lcol_r, lk_ss, lk_rs)
        for c in copies:
            c.start()
        pending += copies

        def stencil(i, carry):
            base = pl.multiple_of(i * RB, RB)
            here = pl.ds(base, RB)
            diag = (1.0 + 4.0 * dispersion - SHIFT) + ld[here, :]
            result = []
            for c in range(2):
                x = vec[e, c, pl.ds(base, RB + 2 * PAD), :]
                mid = x[PAD : PAD + RB, :]
                beside = x[PAD - 1 : PAD - 1 + RB, :] + x[PAD + 1 : PAD + 1 + RB, :]
                beside = beside + from_left(mid) + from_right(mid)
                image = diag * mid - dispersion * beside
                if e < 2:
                    vec[e + 1, c, pl.ds(pl.multiple_of(base + PAD, PAD), RB), :] = image
                for q, term in enumerate((mid * mid, mid * image)):
                    result.append(
                        carry[2 * c + q] + jnp.sum(term.reshape(RB // 8, 8, cols), axis=0)
                    )
            return tuple(result)

        sums = lax.fori_loop(
            0, lrows // RB, stencil, tuple(jnp.zeros((8, cols), f32) for _ in range(4))
        )
        for c in copies:
            c.wait_recv()
        for c in range(2):
            halo_row = [
                jnp.where(there[d], lrow_r[e, d, c : c + 1, :], 0.0) for d in range(2)
            ]
            halo_col = [
                jnp.where(there[2 + d], lcol_r[e, d, c : c + 1, :], 0.0) for d in range(2)
            ]
            edge_r = lrow_s[e, 1, c : c + 1, :] * halo_row[0] + lrow_s[e, 0, c : c + 1, :] * halo_row[1]
            edge_c = lcol_s[e, 1, c : c + 1, :] * halo_col[0] + lcol_s[e, 0, c : c + 1, :] * halo_col[1]
            even = jnp.sum(sums[2 * c], axis=0, keepdims=True)
            odd = jnp.sum(sums[2 * c + 1], axis=0, keepdims=True) - dispersion * edge_r
            even = jnp.sum(even, axis=1, keepdims=True)
            odd = jnp.sum(odd, axis=1, keepdims=True) - dispersion * jnp.sum(
                edge_c, axis=1, keepdims=True
            )
            mine = jnp.where(spot == 6 * c + 2 * e, even, mine)
            mine = jnp.where(spot == 6 * c + 2 * e + 1, odd, mine)
            if e < 2:
                sub = lax.broadcasted_iota(jnp.int32, (8, cols), 0)
                for d, (r0, at_row) in enumerate(((0, 0), (lrows - 8, 7))):
                    vec[e + 1, c, PAD + r0 : PAD + r0 + 8, :] -= jnp.where(
                        sub == at_row, dispersion * halo_row[d], 0.0
                    )
                tile_lane = lax.broadcasted_iota(jnp.int32, (lrows, 128), 1)
                for d, (c0, at_lane) in enumerate(((0, 0), (cols - 128, 127))):
                    vec[e + 1, c, PAD : PAD + lrows, c0 : c0 + 128] -= jnp.where(
                        tile_lane == at_lane, dispersion * as_column(halo_col[d]), 0.0
                    )

    sum_s[...] = mine

    def sum_copy(t, s):
        return pltpu.make_async_remote_copy(
            src_ref=sum_s,
            dst_ref=sum_r.at[s],
            send_sem=sum_ss.at[t],
            recv_sem=sum_rs.at[s],
            device_id=coords(t),
            device_id_type=MESH,
        )

    def send_sums(k, carry):
        sum_copy(peer(k), me).start()
        return carry

    lax.fori_loop(1, n, send_sums, 0)

    for c in pending:
        c.wait_send()

    def sent(k, carry):
        tag_copy(k).wait_send()
        blk_copy(k).wait_send()
        return carry

    lax.fori_loop(1, n, sent, 0)

    def got_sums(k, total):
        s = peer(k)
        sum_copy(s, s).wait_recv()
        return total

    lax.fori_loop(1, n, got_sums, 0)
    sum_r[me] = mine
    total = jnp.sum(sum_r[...], axis=0)

    stores = []
    for c in range(2):
        nu = [
            jnp.sum(jnp.where(spot == 6 * c + k, total, 0.0), axis=1, keepdims=True)
            for k in range(6)
        ]
        hk = [nu[k + 1] + SHIFT * nu[k] for k in range(5)]
        l10 = hk[1] / hk[0]
        l20 = hk[2] / hk[0]
        d1 = hk[2] - l10 * hk[1]
        s21 = hk[3] - l20 * hk[1]
        l21 = s21 / d1
        d2 = hk[4] - l20 * hk[2] - l21 * s21
        y1 = nu[1] - l10 * nu[0]
        y2 = nu[2] - l20 * nu[0] - l21 * y1
        c2 = y2 / d2
        c1 = y1 / d1 - l21 * c2
        c0 = nu[0] / hk[0] - l10 * c1 - l20 * c2

        def combine(i, carry):
            here = pl.ds(pl.multiple_of(i * RB + PAD, PAD), RB)
            vec[0, c, here, :] = (
                c0 * vec[0, c, here, :] + c1 * vec[1, c, here, :] + c2 * vec[2, c, here, :]
            )
            return carry

        lax.fori_loop(0, lrows // RB, combine, 0)
        store = pltpu.make_async_copy(
            vec.at[0, c, pl.ds(PAD, lrows), :], lake_out.at[c], loc.at[c]
        )
        store.start()
        stores.append(store)

    def sent_sums(k, carry):
        sum_copy(peer(k), me).wait_send()
        return carry

    lax.fori_loop(1, n, sent_sums, 0)
    slope_store.wait()
    height_store.wait()
    for store in stores:
        store.wait()


def per_device(
    n0,
    n1,
    slope_depth,
    slope_momentum,
    bed_slope,
    friction,
    slope_active,
    owners,
    offsets,
    lake_height,
    lake_momentum,
    lake_diagonal,
):
    n = n0 * n1
    rows, cols = slope_depth.shape
    lrows = lake_height.shape[0]
    cap = -(-max(2, 2 * rows // n) // 8) * 8
    slots = n * cap
    f32 = jnp.float32
    dma = pltpu.SemaphoreType.DMA
    vmem = pl.BlockSpec(memory_space=pltpu.VMEM)
    hbm = pl.BlockSpec(memory_space=pl.ANY)
    return pl.pallas_call(
        functools.partial(kernel, n0, n1, cap),
        out_shape=(
            jax.ShapeDtypeStruct((3, rows, cols), f32),
            jax.ShapeDtypeStruct((lrows, cols), f32),
            jax.ShapeDtypeStruct((2, lrows, cols), f32),
        ),
        in_specs=[hbm] * 5 + [vmem] * 2 + [hbm] * 3,
        out_specs=(hbm,) * 3,
        scratch_shapes=[
            pltpu.VMEM((SECTIONS + 1, 3, rows + 2 * PAD, cols), f32),
            pltpu.VMEM((3, rows, 3 * cols), jnp.bfloat16),
            pltpu.VMEM((slots, 3 * cols), f32),
            pltpu.VMEM((slots, 3 * cols), f32),
            pltpu.VMEM((slots, 128), f32),
            pltpu.VMEM((slots, 128), f32),
            pltpu.VMEM((slots // 128, lrows, 128), jnp.bfloat16),
            pltpu.VMEM((3, 128, 3 * cols), jnp.bfloat16),
            pltpu.VMEM((2, rows, cols), f32),
            pltpu.VMEM((rows, cols), f32),
            pltpu.VMEM((rows, cols), slope_active.dtype),
            pltpu.VMEM((3, 2, lrows + 2 * PAD, cols), f32),
            pltpu.VMEM((lrows, cols), f32),
            pltpu.VMEM((lrows, cols), f32),
            pltpu.VMEM((SECTIONS, 2, 3, cols), f32),
            pltpu.VMEM((SECTIONS, 2, 3, cols), f32),
            pltpu.VMEM((SECTIONS, 2, 3, rows), f32),
            pltpu.VMEM((SECTIONS, 2, 3, rows), f32),
            pltpu.VMEM((3, 2, 2, cols), f32),
            pltpu.VMEM((3, 2, 2, cols), f32),
            pltpu.VMEM((3, 2, 2, lrows), f32),
            pltpu.VMEM((3, 2, 2, lrows), f32),
            pltpu.VMEM((1, 128), f32),
            pltpu.VMEM((n, 1, 128), f32),
            dma((n,)),
            dma((n,)),
            dma((n,)),
            dma((n,)),
            dma((SECTIONS, 4)),
            dma((SECTIONS, 4)),
            dma((3, 4)),
            dma((3, 4)),
            dma((n,)),
            dma((n,)),
            dma((13,)),
        ],
        compiler_params=pltpu.CompilerParams(
            collective_id=0, has_side_effects=True, vmem_limit_bytes=58 * 1024 * 1024
        ),
    )(
        slope_depth,
        slope_momentum,
        bed_slope,
        friction,
        slope_active,
        owners.reshape(1, rows),
        offsets.reshape(1, rows),
        lake_height,
        lake_momentum,
        lake_diagonal,
    )


def solution(mesh):
    return jax.shard_map(
        functools.partial(per_device, mesh.shape["gx"], mesh.shape["gy"]),
        mesh=mesh,
        in_specs=(
            P("gx", "gy"),
            P(None, "gx", "gy"),
            P(None, "gx", "gy"),
            P("gx", "gy"),
            P("gx", "gy"),
            P("gx", "gy", None, None),
            P("gx", "gy", None),
            P("gx", "gy"),
            P(None, "gx", "gy"),
            P("gx", "gy"),
        ),
        out_specs=(P(None, "gx", "gy"), P("gx", "gy"), P(None, "gx", "gy")),
        check_vma=False,
    )
```
